32 devices in a mesh: parts: 2 (over y), expert: 8 (over z, x), tensor: 2 (over core).
Axes of the slice: x: 2, y: 2, z: 4, core: 2. Of those that a mesh axis runs over, the one named last changes fastest.
Arguments:
- latent_rows: bfloat16 [4096, 1024], P(('parts', 'expert', 'tensor')), parts along dimension 0, may hold values from -6 to 6
- expert_ids: int32 [4096, 4], P(('parts', 'expert', 'tensor')), parts along dimension 0, may hold values from 0 to 7, all different within a row; in each aligned block of 128 rows (0 to 127, 128 to 255, ...) at most 96 rows name the same one
- route_weights: float32 [4096, 4], P(('parts', 'expert', 'tensor')), parts along dimension 0, may hold values from 0.05 to 0.6
- up_weight: bfloat16 [8, 1024, 2048], P('expert', None, 'tensor'), may hold values from -0.1875 to 0.1875
- down_weight: bfloat16 [8, 2048, 1024], P('expert', 'tensor'), may hold values from -0.125 to 0.125
Outputs:
- combined: bfloat16 [4096, 1024], P(('parts', 'expert', 'tensor')), parts along dimension 0
The draws below stay inside these ranges and needn't reach their ends.
There are 2 independent parts, one for each index of `parts`. The reference program is written for one: setup_inputs(seed, part) draws one part's arguments, and reference() takes and returns one part's arrays. A program takes and returns all parts, laid end to end along the dimension named above; an argument that names none is the same for every part. Nothing has to cross between parts.
Inputs may be any that keep to these rules, and one draw needn't show every extreme that they name: `expert_ids`: in each aligned block of 128 rows no expert is named more than 96 times, a bound that some block reaches; the ids of a row differ.
All inputs are finite; a program needn't handle non-finite values.
Results may differ from the reference program's by a relative error of at most 0.0065.
Values may be sent and summed in bfloat16 or wider, within the bound.
No kernel may reach another device: no remote copies, remote signals or barrier semaphores. Data moves between devices by JAX's collectives and lax.ppermute only.
A program may use at most 64 MiB of HBM per device.

```python
import math
import jax
import jax.numpy as jnp
import numpy as np
from jax import lax

L = 1024
H = 2048
TOP = 4
TOK_DEV = 128
EXPERTS = 8
TOKENS = 2048
CAP = 96


def block_scale(own_key, shape, cuts, low, high):
    loudness, own = 1.0, jax.random.fold_in(own_key, 6)
    for dim, parts in cuts:
        steps = jnp.exp(jax.random.uniform(jax.random.fold_in(own, dim), (parts,), jnp.float32, low / len(cuts), high / len(cuts)))
        loudness = loudness * jnp.repeat(steps, shape[dim] // parts).reshape([-1 if axis == dim else 1 for axis in range(len(shape))])
    return loudness


def shared_out(stream_key, own, number, rows, count, top, reach, skew):
    order = jax.random.permutation(stream_key, count)
    packed, ordinary = shares(count, rows * top, reach, skew, True), shares(count, rows * top, reach, skew, False)
    places = jnp.arange(count)

    def named(lengths, offset_by):
        used = int((lengths > 0).sum())
        fixed = max(1, used // 4)
        moved = fixed + (places - fixed + offset_by * (used - fixed)) % max(1, count - fixed)
        return jnp.zeros((count,), jnp.int32).at[order[jnp.where(places < fixed, places, moved)]].set(jnp.asarray(lengths, jnp.int32))

    lengths = jnp.where(number % 4 == 0, named(packed, number // 4), named(ordinary, number - number // 4 - 1))
    mixed = jax.random.permutation(jax.random.fold_in(own, 3), count)
    giver, taker = mixed[0:count // 2 * 2:2], mixed[1:count // 2 * 2:2]
    margin = jnp.minimum(lengths[giver] - 1, reach - lengths[taker]) // 2
    margin = jnp.where((giver == order[0]) | (taker == order[0]) | (lengths[taker] == 0), 0, jnp.maximum(margin, 0))
    moved = jax.random.randint(jax.random.fold_in(own, 4), (count // 2,), 0, 1 << 20) % (margin + 1)
    lengths = lengths.at[giver].add(-moved).at[taker].add(moved)
    items = jnp.searchsorted(jnp.cumsum(lengths), jnp.arange(rows * top), side="right").astype(jnp.int32)
    grid = items.reshape(top, rows).T
    grid = grid[jax.random.permutation(jax.random.fold_in(own, 1), rows)]
    offset_by = jax.random.randint(jax.random.fold_in(own, 2), (rows, 1), 0, top)
    return jnp.take_along_axis(grid, (jnp.arange(top)[None, :] + offset_by) % top, axis=1)


def shares(count, total, limit, slope, full):
    weights = [(1 << 20) // math.isqrt(grade ** slope) + 1 for grade in range(1, count + 1)]
    largest = limit if full else min(limit, max(-(-total // count), total * weights[0] // sum(weights)))
    least = 1 if total - largest >= count - 1 else 0
    counts, surplus = [largest] + [least] * (count - 1), total - largest - least * (count - 1)
    while surplus > 0:
        candidates = [i for i in range(1, count) if counts[i] < largest] or [i for i in range(1, count) if counts[i] < limit]
        mass, budget = sum([weights[i] for i in candidates]), surplus
        for i in candidates:
            addition = min(limit - counts[i], max(1, budget * weights[i] // mass), surplus)
            counts[i] = counts[i] + addition
            surplus = surplus - addition
    return np.array(counts)


def gaussian(rng, extent, scale, reach, split=(), kind=jnp.bfloat16):
    gain = block_scale(rng, extent, split, -0.22, 0.18) if split else 1.0
    drawn = jax.random.normal(rng, extent, jnp.float32) * scale * gain
    return jnp.minimum(jnp.maximum(drawn, -reach), reach).astype(kind)


def setup_inputs(seed: int = 0, part: int = 0) -> dict:
    keys = jax.random.split(jax.random.key(seed), 6)
    part_splits = jax.random.split(jax.random.fold_in(keys[5], part), 6)
    latent_rows = gaussian(part_splits[0], (TOKENS, L), 1.0, 6.0, ((0, 16),))
    expert_ids_keys = jax.random.split(jax.random.fold_in(part_splits[1], 1), TOKENS // TOK_DEV)
    expert_ids_turns = jax.random.permutation(jax.random.fold_in(part_splits[1], 3), TOKENS // TOK_DEV)
    expert_ids = jax.vmap(lambda own, number: shared_out(jax.random.fold_in(part_splits[1], 2), own, number, TOK_DEV, EXPERTS, TOP, CAP, 2))(expert_ids_keys, expert_ids_turns).reshape((TOKENS, TOP))
    route_weights = jnp.clip(0.05 + 0.55 * jax.random.uniform(part_splits[2], (TOKENS, TOP), jnp.float32) ** block_scale(part_splits[2], (TOKENS, TOP), ((0, 16),), -0.2, 0.2), 0.05, 0.6)
    up_weight = gaussian(keys[3], (EXPERTS, L, H), L ** -0.5, 0.1875, ((0, 8), (2, 2)))
    down_weight = gaussian(keys[4], (EXPERTS, H, L), H ** -0.5, 0.125, ((0, 8), (1, 2)))
    return dict(latent_rows=latent_rows, expert_ids=expert_ids, route_weights=route_weights, up_weight=up_weight, down_weight=down_weight)


def reference(latent_rows, expert_ids, route_weights, up_weight, down_weight):
    blocks = TOKENS // TOK_DEV
    per_block = TOK_DEV * TOP
    flat_ids = expert_ids.reshape(blocks, per_block)
    onehot = (flat_ids[:, :, None] == jnp.arange(EXPERTS, dtype=jnp.int32)[None, None, :]).astype(jnp.int32)
    ranks = jnp.cumsum(onehot, axis=1) - onehot
    slots = jnp.sum(ranks * onehot, axis=2)
    total = TOKENS * TOP
    assign = jnp.arange(total, dtype=jnp.int32).reshape(blocks, per_block)
    column = jnp.arange(blocks, dtype=jnp.int32)[:, None] * CAP + slots
    table = jnp.full((EXPERTS, blocks * CAP), total, jnp.int32)
    table = table.at[flat_ids.reshape(-1), column.reshape(-1)].set(assign.reshape(-1))
    rows_all = jnp.concatenate([jnp.repeat(latent_rows, TOP, axis=0), jnp.zeros((1, L), jnp.bfloat16)], axis=0)
    weight_all = jnp.concatenate([route_weights.reshape(-1), jnp.zeros((1,), jnp.float32)])
    half = H // 2

    def one_expert(acc, inputs):
        index, w_up, w_down = inputs
        picked = rows_all[index]
        pre = jnp.dot(picked, w_up, preferred_element_type=jnp.float32)
        hidden = (jnp.maximum(pre, 0.0) ** 2).astype(jnp.bfloat16)
        first = jnp.dot(hidden[:, :half], w_down[:half], preferred_element_type=jnp.float32).astype(jnp.bfloat16)
        second = jnp.dot(hidden[:, half:], w_down[half:], preferred_element_type=jnp.float32).astype(jnp.bfloat16)
        result = (first.astype(jnp.float32) + second.astype(jnp.float32)).astype(jnp.bfloat16)
        term = weight_all[index][:, None] * result.astype(jnp.float32)
        acc = acc.at[index // TOP].add(term)
        return acc, None

    start = jnp.zeros((TOKENS + 1, L), jnp.float32)
    acc, unused = lax.scan(one_expert, start, (table, up_weight, down_weight))
    return acc[:TOKENS].astype(jnp.bfloat16)
```

```python
import jax
import jax.numpy as jnp
from jax import lax
from jax.sharding import PartitionSpec as P


def exchange_body(latent_rows, expert_ids, route_weights, up_weight, down_weight):
    rows_dev = latent_rows.shape[0]
    width = latent_rows.shape[1]
    choose = expert_ids.shape[1]
    groups = lax.axis_size("expert")
    capacity = 3 * choose * rows_dev // (2 * groups)
    flat_ids = expert_ids.reshape(-1)
    onehot = (flat_ids[:, None] == jnp.arange(groups, dtype=jnp.int32)[None, :]).astype(jnp.int32)
    ranks = jnp.cumsum(onehot, axis=0) - onehot
    slots = jnp.sum(ranks * onehot, axis=1)
    target = flat_ids * capacity + slots
    repeated = jnp.repeat(latent_rows, choose, axis=0)
    outgoing = jnp.zeros((groups * capacity, width), jnp.bfloat16).at[target].set(repeated)
    outgoing = outgoing.reshape(groups, capacity, width)
    arrived = lax.all_to_all(outgoing, "expert", split_axis=0, concat_axis=0, tiled=True)
    arrived_rows = arrived.reshape(-1, width)
    both_rows = lax.all_gather(arrived_rows, "tensor", axis=0, tiled=True)
    pre = jnp.dot(both_rows, up_weight[0], preferred_element_type=jnp.float32)
    hidden = (jnp.maximum(pre, 0.0) ** 2).astype(jnp.bfloat16)
    partial_out = jnp.dot(hidden, down_weight[0], preferred_element_type=jnp.float32)
    summed = lax.psum_scatter(
        partial_out.astype(jnp.bfloat16), "tensor", scatter_dimension=0, tiled=True
    )
    returned = lax.all_to_all(
        summed.reshape(groups, capacity, width), "expert", split_axis=0, concat_axis=0, tiled=True
    )
    returned_rows = returned.reshape(-1, width)
    picked = returned_rows[target].astype(jnp.float32)
    weighted = picked * route_weights.reshape(-1)[:, None]
    combined = jnp.sum(weighted.reshape(rows_dev, choose, width), axis=1)
    return combined.astype(jnp.bfloat16)


def across(value, step):
    size = lax.axis_size("expert")
    return lax.ppermute(value, "expert", [(i, i ^ step) for i in range(size)])


def other_core(value):
    return lax.ppermute(value, "tensor", [(0, 1), (1, 0)])


def gather_body(latent_rows, expert_ids, route_weights, up_weight, down_weight):
    groups = lax.axis_size("expert")
    me = lax.axis_index("expert")
    core = lax.axis_index("tensor")
    f32 = jnp.float32
    chosen = expert_ids[None, :, :] == jnp.arange(groups, dtype=jnp.int32)[:, None, None]
    table = jnp.sum(jnp.where(chosen, route_weights[None], 0.0), axis=2)
    tables = lax.all_gather(table, ("expert", "tensor"), axis=0, tiled=False)
    mine = lax.dynamic_index_in_dim(tables, me, axis=1, keepdims=False)
    near = [latent_rows] + [across(latent_rows, 2 * k) for k in range(1, groups // 2)]
    far = [across(rows, 1) for rows in near]

    def weights_of(step, swap):
        place = (me ^ step) * 2 + (core ^ swap)
        return lax.dynamic_index_in_dim(mine, place, axis=0, keepdims=False)

    def core_sum(rows, step):
        both = jnp.concatenate([rows, other_core(rows)], axis=0)
        weight = jnp.concatenate([weights_of(step, 0), weights_of(step, 1)])
        pre = jnp.dot(both, up_weight[0], preferred_element_type=f32)
        hidden = jnp.square(jnp.maximum(pre, 0.0)).astype(jnp.bfloat16)
        out = jnp.dot(hidden, down_weight[0], preferred_element_type=f32)
        out = (out * weight[:, None]).astype(jnp.bfloat16)
        n = rows.shape[0]
        return out[:n].astype(f32), other_core(out[n:]).astype(f32)

    total = None
    for k in [*range(1, groups // 2), 0]:
        a, b = core_sum(far[k], 2 * k + 1)
        over = across((a + b).astype(jnp.bfloat16), 1).astype(f32)
        a, b = core_sum(near[k], 2 * k)
        part = a + b + over
        if k:
            part = across(part.astype(jnp.bfloat16), 2 * k).astype(f32)
        total = part if total is None else total + part
    return total.astype(jnp.bfloat16)


def body(latent_rows, expert_ids, route_weights, up_weight, down_weight):
    groups = lax.axis_size("expert")
    rows_dev, choose = expert_ids.shape
    capacity = 3 * choose * rows_dev // (2 * groups)
    dense = rows_dev <= 2 * capacity and groups & (groups - 1) == 0
    form = gather_body if dense else exchange_body
    return form(latent_rows, expert_ids, route_weights, up_weight, down_weight)


def solution(mesh):
    return jax.shard_map(
        body,
        mesh=mesh,
        in_specs=(
            P(("parts", "expert", "tensor"), None),
            P(("parts", "expert", "tensor"), None),
            P(("parts", "expert", "tensor"), None),
            P("expert", None, "tensor"),
            P("expert", "tensor", None),
        ),
        out_specs=P(("parts", "expert", "tensor"), None),
        check_vma=False,
    )
```

```python
import jax
import jax.numpy as jnp
from jax import lax
from jax.experimental import pallas as pl
from jax.experimental.pallas import tpu as pltpu
from jax.sharding import PartitionSpec as P


def exchange_body(latent_rows, expert_ids, route_weights, up_weight, down_weight):
    rows_dev = latent_rows.shape[0]
    width = latent_rows.shape[1]
    choose = expert_ids.shape[1]
    groups = lax.axis_size("expert")
    capacity = 3 * choose * rows_dev // (2 * groups)
    flat_ids = expert_ids.reshape(-1)
    onehot = (flat_ids[:, None] == jnp.arange(groups, dtype=jnp.int32)[None, :]).astype(jnp.int32)
    ranks = jnp.cumsum(onehot, axis=0) - onehot
    slots = jnp.sum(ranks * onehot, axis=1)
    target = flat_ids * capacity + slots
    repeated = jnp.repeat(latent_rows, choose, axis=0)
    outgoing = jnp.zeros((groups * capacity, width), jnp.bfloat16).at[target].set(repeated)
    outgoing = outgoing.reshape(groups, capacity, width)
    arrived = lax.all_to_all(outgoing, "expert", split_axis=0, concat_axis=0, tiled=True)
    arrived_rows = arrived.reshape(-1, width)
    both_rows = lax.all_gather(arrived_rows, "tensor", axis=0, tiled=True)
    pre = jnp.dot(both_rows, up_weight[0], preferred_element_type=jnp.float32)
    hidden = (jnp.maximum(pre, 0.0) ** 2).astype(jnp.bfloat16)
    partial_out = jnp.dot(hidden, down_weight[0], preferred_element_type=jnp.float32)
    summed = lax.psum_scatter(
        partial_out.astype(jnp.bfloat16), "tensor", scatter_dimension=0, tiled=True
    )
    returned = lax.all_to_all(
        summed.reshape(groups, capacity, width), "expert", split_axis=0, concat_axis=0, tiled=True
    )
    returned_rows = returned.reshape(-1, width)
    picked = returned_rows[target].astype(jnp.float32)
    weighted = picked * route_weights.reshape(-1)[:, None]
    combined = jnp.sum(weighted.reshape(rows_dev, choose, width), axis=1)
    return combined.astype(jnp.bfloat16)


def across(value, step):
    size = lax.axis_size("expert")
    return lax.ppermute(value, "expert", [(i, i ^ step) for i in range(size)])


def other_core(value):
    return lax.ppermute(value, "tensor", [(0, 1), (1, 0)])


def expert_kernel(near, far, choice, up_a, down_a, up_b, down_b, near_out, far_out):
    f32 = jnp.float32
    n = near_out.shape[0]
    blocks = [near[...], far[...]]
    rows = jnp.concatenate([b[:n] for b in blocks], axis=0)
    total = None
    for up, down in ((up_a, down_a), (up_b, down_b)):
        pre = jnp.dot(rows, up[...], preferred_element_type=f32)
        hidden = jnp.square(jnp.maximum(pre, 0.0)).astype(jnp.bfloat16)
        out = jnp.dot(hidden, down[...], preferred_element_type=f32)
        total = out if total is None else total + out
    for i, ref in enumerate((near_out, far_out)):
        pair = blocks[i][n:, : 2 * n].astype(f32)
        weight = jnp.sum((pair[:, :n] + pair[:, n:]) * choice[...], axis=0, keepdims=True)
        column = jnp.broadcast_to(weight, (n, n)).T
        for c in range(0, ref.shape[1], n):
            ref[:, c : c + n] = (total[i * n : (i + 1) * n, c : c + n] * column).astype(ref.dtype)


def expert(near, far, choice, weights, n):
    width = near.shape[1]
    units = weights[0].shape[1]
    return pl.pallas_call(
        expert_kernel,
        out_shape=[
            jax.ShapeDtypeStruct((n, width), jnp.float32),
            jax.ShapeDtypeStruct((n, width), jnp.bfloat16),
        ],
        in_specs=[pl.BlockSpec(memory_space=pltpu.VMEM)] * 7,
        out_specs=[pl.BlockSpec(memory_space=pltpu.VMEM)] * 2,
        compiler_params=pltpu.CompilerParams(vmem_limit_bytes=40 << 20),
        cost_estimate=pl.CostEstimate(
            flops=16 * n * width * units, bytes_accessed=8 * width * units, transcendentals=0
        ),
    )(near, far, choice, *weights)


def gather_body(latent_rows, expert_ids, route_weights, up_weight, down_weight):
    groups = lax.axis_size("expert")
    n, width = latent_rows.shape
    me = lax.axis_index("expert")
    f32 = jnp.float32
    names = jnp.arange(groups, dtype=jnp.int32)
    chosen = expert_ids[None, :, :] == names[:, None, None]
    table = jnp.sum(jnp.where(chosen, route_weights[None], 0.0), axis=2)
    high = lax.reduce_precision(table, 8, 7)
    strip = jnp.concatenate([high, table - high], axis=1).astype(jnp.bfloat16)
    strip = jnp.pad(strip, ((0, 0), (0, width - 2 * n)))
    choice = jnp.broadcast_to((names == me).astype(f32)[:, None], (groups, n))

    near = {0: jnp.concatenate([latent_rows, strip], axis=0)}
    far = {0: across(near[0], 1)}
    for k in range(1, groups // 2):
        low = k & -k
        near[k] = across(near[k ^ low], 2 * low)
        far[k] = across(near[k], 1)
    weights = (up_weight[0], down_weight[0], other_core(up_weight[0]), other_core(down_weight[0]))

    own, away = {}, {}
    for k in range(groups // 2):
        own[k], away[k] = expert(near[k], far[k], choice, weights, n)
    sums = {}
    for k in reversed(range(groups // 2)):
        sums[k] = own[k] + across(away[k], 1).astype(f32)
    for k in reversed(range(1, groups // 2)):
        low = k & -k
        sums[k ^ low] = sums[k ^ low] + across(sums[k].astype(jnp.bfloat16), 2 * low).astype(f32)
    return sums[0].astype(jnp.bfloat16)


def body(latent_rows, expert_ids, route_weights, up_weight, down_weight):
    groups = lax.axis_size("expert")
    rows_dev, choose = expert_ids.shape
    capacity = 3 * choose * rows_dev // (2 * groups)
    dense = rows_dev <= 2 * capacity and groups & (groups - 1) == 0
    form = gather_body if dense else exchange_body
    return form(latent_rows, expert_ids, route_weights, up_weight, down_weight)


def solution(mesh):
    return jax.shard_map(
        body,
        mesh=mesh,
        in_specs=(
            P(("parts", "expert", "tensor"), None),
            P(("parts", "expert", "tensor"), None),
            P(("parts", "expert", "tensor"), None),
            P("expert", None, "tensor"),
            P("expert", "tensor", None),
        ),
        out_specs=P(("parts", "expert", "tensor"), None),
        check_vma=False,
    )
```

```python
import jax
import jax.numpy as jnp
from jax import lax
from jax.experimental import pallas as pl
from jax.experimental.pallas import tpu as pltpu
from jax.sharding import PartitionSpec as P


def exchange_body(latent_rows, expert_ids, route_weights, up_weight, down_weight):
    rows_dev = latent_rows.shape[0]
    width = latent_rows.shape[1]
    choose = expert_ids.shape[1]
    groups = lax.axis_size("expert")
    capacity = 3 * choose * rows_dev // (2 * groups)
    flat_ids = expert_ids.reshape(-1)
    onehot = (flat_ids[:, None] == jnp.arange(groups, dtype=jnp.int32)[None, :]).astype(jnp.int32)
    ranks = jnp.cumsum(onehot, axis=0) - onehot
    slots = jnp.sum(ranks * onehot, axis=1)
    target = flat_ids * capacity + slots
    repeated = jnp.repeat(latent_rows, choose, axis=0)
    outgoing = jnp.zeros((groups * capacity, width), jnp.bfloat16).at[target].set(repeated)
    outgoing = outgoing.reshape(groups, capacity, width)
    arrived = lax.all_to_all(outgoing, "expert", split_axis=0, concat_axis=0, tiled=True)
    arrived_rows = arrived.reshape(-1, width)
    both_rows = lax.all_gather(arrived_rows, "tensor", axis=0, tiled=True)
    pre = jnp.dot(both_rows, up_weight[0], preferred_element_type=jnp.float32)
    hidden = (jnp.maximum(pre, 0.0) ** 2).astype(jnp.bfloat16)
    partial_out = jnp.dot(hidden, down_weight[0], preferred_element_type=jnp.float32)
    summed = lax.psum_scatter(
        partial_out.astype(jnp.bfloat16), "tensor", scatter_dimension=0, tiled=True
    )
    returned = lax.all_to_all(
        summed.reshape(groups, capacity, width), "expert", split_axis=0, concat_axis=0, tiled=True
    )
    returned_rows = returned.reshape(-1, width)
    picked = returned_rows[target].astype(jnp.float32)
    weighted = picked * route_weights.reshape(-1)[:, None]
    combined = jnp.sum(weighted.reshape(rows_dev, choose, width), axis=1)
    return combined.astype(jnp.bfloat16)


def across(value, step):
    size = lax.axis_size("expert")
    return lax.ppermute(value, "expert", [(i, i ^ step) for i in range(size)])


def other_core(value):
    return lax.ppermute(value, "tensor", [(0, 1), (1, 0)])


def after(value, *others):
    return lax.optimization_barrier((value, *others))[0]


def expert_kernel(near, far, choice, up_a, down_a, up_b, down_b, near_out, far_out):
    f32 = jnp.float32
    n = near_out.shape[0]
    blocks = [near[...], far[...]]
    rows = jnp.concatenate([b[:n] for b in blocks], axis=0)
    total = None
    for up, down in ((up_a, down_a), (up_b, down_b)):
        pre = jnp.dot(rows, up[...], preferred_element_type=f32)
        hidden = jnp.square(jnp.maximum(pre, 0.0)).astype(jnp.bfloat16)
        out = jnp.dot(hidden, down[...], preferred_element_type=f32)
        total = out if total is None else total + out
    for i, ref in enumerate((near_out, far_out)):
        pair = blocks[i][n:, : 2 * n].astype(f32)
        weight = jnp.sum((pair[:, :n] + pair[:, n:]) * choice[...], axis=0, keepdims=True)
        column = jnp.broadcast_to(weight, (n, n)).T
        for c in range(0, ref.shape[1], n):
            ref[:, c : c + n] = (total[i * n : (i + 1) * n, c : c + n] * column).astype(ref.dtype)


def expert(near, far, choice, weights, n):
    width = near.shape[1]
    units = weights[0].shape[1]
    return pl.pallas_call(
        expert_kernel,
        out_shape=[
            jax.ShapeDtypeStruct((n, width), jnp.float32),
            jax.ShapeDtypeStruct((n, width), jnp.bfloat16),
        ],
        in_specs=[pl.BlockSpec(memory_space=pltpu.VMEM)] * 7,
        out_specs=[pl.BlockSpec(memory_space=pltpu.VMEM)] * 2,
        compiler_params=pltpu.CompilerParams(vmem_limit_bytes=20 << 20),
        cost_estimate=pl.CostEstimate(
            flops=n * width, bytes_accessed=n * width, transcendentals=0
        ),
    )(near, far, choice, *weights)


def gather_body(latent_rows, expert_ids, route_weights, up_weight, down_weight):
    groups = lax.axis_size("expert")
    n, width = latent_rows.shape
    me = lax.axis_index("expert")
    f32 = jnp.float32
    names = jnp.arange(groups, dtype=jnp.int32)
    chosen = expert_ids[None, :, :] == names[:, None, None]
    table = jnp.sum(jnp.where(chosen, route_weights[None], 0.0), axis=2)
    high = lax.reduce_precision(table, 8, 7)
    strip = jnp.concatenate([high, table - high], axis=1).astype(jnp.bfloat16)
    strip = jnp.pad(strip, ((0, 0), (0, width - 2 * n)))
    choice = jnp.broadcast_to((names == me).astype(f32)[:, None], (groups, n))

    near, far, own, away, over = {}, {}, {}, {}, {}

    def run(k):
        own[k], away[k] = expert(near[k], far[k], choice, weights, n)

    near[0] = jnp.concatenate([latent_rows, strip], axis=0)
    far[0] = across(near[0], 1)
    near[2] = across(near[0], 4)
    weights = (up_weight[0], down_weight[0], other_core(up_weight[0]), other_core(down_weight[0]))
    near[2] = after(near[2], far[0])
    near[3] = across(near[2], 2)
    far[2] = across(near[2], 1)
    run(0)
    near[1] = across(after(near[0], near[2]), 2)
    far[1] = across(after(far[0], near[2]), 2)
    near[3] = after(near[3], far[2], away[0])
    far[3] = across(near[3], 1)
    run(2)
    near[3] = after(near[3], away[2], near[1])
    run(3)
    near[1] = after(near[1], away[3])
    run(1)
    over[3] = across(away[3], 1)
    over[2] = across(after(away[2], away[3]), 1)
    over[1] = across(after(away[1], over[3]), 1)
    over[0] = across(after(away[0], away[1]), 1)
    sums = {k: own[k] + over[k].astype(f32) for k in range(4)}
    sums[2] = sums[2] + across(sums[3].astype(jnp.bfloat16), 2).astype(f32)
    sums[0] = sums[0] + across(sums[1].astype(jnp.bfloat16), 2).astype(f32)
    sums[0] = sums[0] + across(sums[2].astype(jnp.bfloat16), 4).astype(f32)
    return sums[0].astype(jnp.bfloat16)


def body(latent_rows, expert_ids, route_weights, up_weight, down_weight):
    groups = lax.axis_size("expert")
    rows_dev, choose = expert_ids.shape
    capacity = 3 * choose * rows_dev // (2 * groups)
    dense = groups == 8 and rows_dev <= 2 * capacity
    form = gather_body if dense else exchange_body
    return form(latent_rows, expert_ids, route_weights, up_weight, down_weight)


def solution(mesh):
    return jax.shard_map(
        body,
        mesh=mesh,
        in_specs=(
            P(("parts", "expert", "tensor"), None),
            P(("parts", "expert", "tensor"), None),
            P(("parts", "expert", "tensor"), None),
            P("expert", None, "tensor"),
            P("expert", "tensor", None),
        ),
        out_specs=P(("parts", "expert", "tensor"), None),
        check_vma=False,
    )
```

```python
import functools

import jax
import jax.numpy as jnp
from jax import lax
from jax.experimental import pallas as pl
from jax.experimental.pallas import tpu as pltpu
from jax.sharding import PartitionSpec as P


def exchange_body(latent_rows, expert_ids, route_weights, up_weight, down_weight):
    rows_dev = latent_rows.shape[0]
    width = latent_rows.shape[1]
    choose = expert_ids.shape[1]
    groups = lax.axis_size("expert")
    capacity = 3 * choose * rows_dev // (2 * groups)
    flat_ids = expert_ids.reshape(-1)
    onehot = (flat_ids[:, None] == jnp.arange(groups, dtype=jnp.int32)[None, :]).astype(jnp.int32)
    ranks = jnp.cumsum(onehot, axis=0) - onehot
    slots = jnp.sum(ranks * onehot, axis=1)
    target = flat_ids * capacity + slots
    repeated = jnp.repeat(latent_rows, choose, axis=0)
    outgoing = jnp.zeros((groups * capacity, width), jnp.bfloat16).at[target].set(repeated)
    outgoing = outgoing.reshape(groups, capacity, width)
    arrived = lax.all_to_all(outgoing, "expert", split_axis=0, concat_axis=0, tiled=True)
    arrived_rows = arrived.reshape(-1, width)
    both_rows = lax.all_gather(arrived_rows, "tensor", axis=0, tiled=True)
    pre = jnp.dot(both_rows, up_weight[0], preferred_element_type=jnp.float32)
    hidden = (jnp.maximum(pre, 0.0) ** 2).astype(jnp.bfloat16)
    partial_out = jnp.dot(hidden, down_weight[0], preferred_element_type=jnp.float32)
    summed = lax.psum_scatter(
        partial_out.astype(jnp.bfloat16), "tensor", scatter_dimension=0, tiled=True
    )
    returned = lax.all_to_all(
        summed.reshape(groups, capacity, width), "expert", split_axis=0, concat_axis=0, tiled=True
    )
    returned_rows = returned.reshape(-1, width)
    picked = returned_rows[target].astype(jnp.float32)
    weighted = picked * route_weights.reshape(-1)[:, None]
    combined = jnp.sum(weighted.reshape(rows_dev, choose, width), axis=1)
    return combined.astype(jnp.bfloat16)


def across(value, step):
    size = lax.axis_size("expert")
    return lax.ppermute(value, "expert", [(i, i ^ step) for i in range(size)])


def other_core(value):
    return lax.ppermute(value, "tensor", [(0, 1), (1, 0)])


def after(value, *others):
    return lax.optimization_barrier((value, *others))[0]


def pack_kernel(rows, ids, weights, out):
    n, width = rows.shape
    lines = []
    for e in range(out.shape[0] - n):
        lines.append(jnp.sum(jnp.where(ids[...] == e, weights[...], 0.0), axis=0, keepdims=True))
    table = jnp.concatenate(lines, axis=0)
    high = table.astype(jnp.bfloat16)
    low = (table - high.astype(jnp.float32)).astype(jnp.bfloat16)
    rest = jnp.zeros((len(lines), width - 2 * n), jnp.bfloat16)
    out[...] = jnp.concatenate([rows[...], jnp.concatenate([high, low, rest], axis=1)], axis=0)


def expert_kernel(counts, *refs):
    f32 = jnp.float32
    near, refs = refs[: counts[0]], refs[counts[0] :]
    far, refs = refs[: counts[0]], refs[counts[0] :]
    choice, up_a, down_a, up_b, down_b = refs[:5]
    own, away, kept = refs[5 : 5 + counts[1]], refs[5 + counts[1] : 5 + 2 * counts[1]], refs[5 + 2 * counts[1] :]
    n = sum(ref.shape[0] for ref in own)
    blocks = [jnp.concatenate([ref[...] for ref in side], axis=0) for side in (near, far)]
    rows = jnp.concatenate([b[:n] for b in blocks], axis=0)
    total = None
    for up, down in ((up_a, down_a), (up_b, down_b)):
        pre = jnp.dot(rows, up[...], preferred_element_type=f32)
        hidden = jnp.square(jnp.maximum(pre, 0.0)).astype(jnp.bfloat16)
        out = jnp.dot(hidden, down[...], preferred_element_type=f32)
        total = out if total is None else total + out
    for i, side in enumerate((own, away)):
        pair = blocks[i][n:, : 2 * n].astype(f32)
        weight = jnp.sum((pair[:, :n] + pair[:, n:]) * choice[...], axis=0, keepdims=True)
        column = jnp.broadcast_to(weight, (n, n)).T
        first = 0
        for ref in side:
            last = first + ref.shape[0]
            for c in range(0, ref.shape[1], n):
                piece = total[i * n + first : i * n + last, c : c + n] * column[first:last]
                ref[:, c : c + n] = piece.astype(ref.dtype)
            first = last
    for ref in kept:
        ref[...] = down_b[...]


def expert(near, far, choice, weights, n, pieces=1, keep=False):
    width = near[0].shape[1]
    out = [jax.ShapeDtypeStruct((n // pieces, width), jnp.float32)] * pieces
    out += [jax.ShapeDtypeStruct((n // pieces, width), jnp.bfloat16)] * pieces
    out += [jax.ShapeDtypeStruct(weights[3].shape, jnp.bfloat16)] * keep
    return pl.pallas_call(
        functools.partial(expert_kernel, (len(near), pieces)),
        out_shape=out,
        in_specs=[pl.BlockSpec(memory_space=pltpu.VMEM)] * (2 * len(near) + 5),
        out_specs=[pl.BlockSpec(memory_space=pltpu.VMEM)] * len(out),
        compiler_params=pltpu.CompilerParams(vmem_limit_bytes=20 << 20),
        cost_estimate=pl.CostEstimate(flops=n * width, bytes_accessed=n * width, transcendentals=0),
    )(*near, *far, choice, *weights)


def gather_body(latent_rows, expert_ids, route_weights, up_weight, down_weight):
    groups = lax.axis_size("expert")
    n, width = latent_rows.shape
    me = lax.axis_index("expert")
    f32 = jnp.float32
    choice = jnp.broadcast_to((jnp.arange(groups) == me).astype(f32)[:, None], (groups, n))
    whole = pl.pallas_call(
        pack_kernel,
        out_shape=jax.ShapeDtypeStruct((n + groups, width), jnp.bfloat16),
        in_specs=[pl.BlockSpec(memory_space=pltpu.VMEM)] * 3,
        out_specs=pl.BlockSpec(memory_space=pltpu.VMEM),
    )(latent_rows, expert_ids.T, route_weights.T)
    near2 = across(whole, 4)
    far0 = across(whole, 1)
    near1 = across(whole, 2)
    weights = (up_weight[0], down_weight[0], other_core(up_weight[0]), other_core(down_weight[0]))
    far3 = across(near2, 3)
    near3 = across(near2, 2)
    far2 = across(near2, 1)
    far0 = after(far0, near2)
    own0, away0, kept = expert([whole], [far0], choice, weights, n, keep=True)
    weights = weights[:3] + (kept,)
    near3, far2, far3 = lax.optimization_barrier((near3, far2, far3, away0, near1))[:3]
    own2, away2 = expert([near2], [far2], choice, weights, n)
    far1 = across(after(far0, near3), 2)
    near3 = after(near3, away2)
    own3, away3 = expert([near3], [far3], choice, weights, n)

    def add(*terms):
        return functools.reduce(lambda a, b: a + b.astype(f32), terms).astype(jnp.bfloat16)

    over2 = across(away2, 1)
    over3 = across(away3, 1)
    near1 = after(near1, away3)
    own1, away1 = expert([near1], [far1], choice, weights, n)
    over1 = across(away1, 1)
    over0 = across(after(away0, over2), 1)
    low3 = across(add(own3, over3), 2)
    sum2 = add(own2, over2, low3)
    high = across(sum2, 4)
    low1 = across(add(own1, after(over1, sum2)), 2)
    return add(own0, over0, low1, high)


def body(latent_rows, expert_ids, route_weights, up_weight, down_weight):
    groups = lax.axis_size("expert")
    rows_dev, choose = expert_ids.shape
    capacity = 3 * choose * rows_dev // (2 * groups)
    dense = groups == 8 and rows_dev <= 2 * capacity
    form = gather_body if dense else exchange_body
    return form(latent_rows, expert_ids, route_weights, up_weight, down_weight)


def solution(mesh):
    return jax.shard_map(
        body,
        mesh=mesh,
        in_specs=(
            P(("parts", "expert", "tensor"), None),
            P(("parts", "expert", "tensor"), None),
            P(("parts", "expert", "tensor"), None),
            P("expert", None, "tensor"),
            P("expert", "tensor", None),
        ),
        out_specs=P(("parts", "expert", "tensor"), None),
        check_vma=False,
    )
```

```python
import functools

import jax
import jax.numpy as jnp
from jax import lax
from jax.experimental import pallas as pl
from jax.experimental.pallas import tpu as pltpu
from jax.sharding import PartitionSpec as P


def exchange_body(latent_rows, expert_ids, route_weights, up_weight, down_weight):
    rows_dev = latent_rows.shape[0]
    width = latent_rows.shape[1]
    choose = expert_ids.shape[1]
    groups = lax.axis_size("expert")
    capacity = 3 * choose * rows_dev // (2 * groups)
    flat_ids = expert_ids.reshape(-1)
    onehot = (flat_ids[:, None] == jnp.arange(groups, dtype=jnp.int32)[None, :]).astype(jnp.int32)
    ranks = jnp.cumsum(onehot, axis=0) - onehot
    slots = jnp.sum(ranks * onehot, axis=1)
    target = flat_ids * capacity + slots
    repeated = jnp.repeat(latent_rows, choose, axis=0)
    outgoing = jnp.zeros((groups * capacity, width), jnp.bfloat16).at[target].set(repeated)
    outgoing = outgoing.reshape(groups, capacity, width)
    arrived = lax.all_to_all(outgoing, "expert", split_axis=0, concat_axis=0, tiled=True)
    arrived_rows = arrived.reshape(-1, width)
    both_rows = lax.all_gather(arrived_rows, "tensor", axis=0, tiled=True)
    pre = jnp.dot(both_rows, up_weight[0], preferred_element_type=jnp.float32)
    hidden = (jnp.maximum(pre, 0.0) ** 2).astype(jnp.bfloat16)
    partial_out = jnp.dot(hidden, down_weight[0], preferred_element_type=jnp.float32)
    summed = lax.psum_scatter(
        partial_out.astype(jnp.bfloat16), "tensor", scatter_dimension=0, tiled=True
    )
    returned = lax.all_to_all(
        summed.reshape(groups, capacity, width), "expert", split_axis=0, concat_axis=0, tiled=True
    )
    returned_rows = returned.reshape(-1, width)
    picked = returned_rows[target].astype(jnp.float32)
    weighted = picked * route_weights.reshape(-1)[:, None]
    combined = jnp.sum(weighted.reshape(rows_dev, choose, width), axis=1)
    return combined.astype(jnp.bfloat16)


def across(value, step):
    size = lax.axis_size("expert")
    return lax.ppermute(value, "expert", [(i, i ^ step) for i in range(size)])


def other_core(value):
    return lax.ppermute(value, "tensor", [(0, 1), (1, 0)])


def after(value, *others):
    return lax.optimization_barrier((value, *others))[0]


def pack_kernel(rows, ids, weights, out):
    n, width = rows.shape
    lines = []
    for e in range(out.shape[0] - n):
        lines.append(jnp.sum(jnp.where(ids[...] == e, weights[...], 0.0), axis=0, keepdims=True))
    table = jnp.concatenate(lines, axis=0)
    high = table.astype(jnp.bfloat16)
    low = (table - high.astype(jnp.float32)).astype(jnp.bfloat16)
    rest = jnp.zeros((len(lines), width - 2 * n), jnp.bfloat16)
    out[...] = jnp.concatenate([rows[...], jnp.concatenate([high, low, rest], axis=1)], axis=0)


def expert_kernel(count, *refs):
    f32 = jnp.float32
    blocks = [ref[...] for ref in refs[:count]]
    choice, up_a, down_a, up_b, down_b = refs[count : count + 5]
    outs, kept = refs[count + 5 : 2 * count + 5], refs[2 * count + 5 :]
    n = outs[0].shape[0]
    rows = jnp.concatenate([b[:n] for b in blocks], axis=0)
    total = None
    for up, down in ((up_a, down_a), (up_b, down_b)):
        pre = jnp.dot(rows, up[...], preferred_element_type=f32)
        hidden = jnp.square(jnp.maximum(pre, 0.0)).astype(jnp.bfloat16)
        out = jnp.dot(hidden, down[...], preferred_element_type=f32)
        total = out if total is None else total + out
    for i, ref in enumerate(outs):
        pair = blocks[i][n:, : 2 * n].astype(f32)
        weight = jnp.sum((pair[:, :n] + pair[:, n:]) * choice[...], axis=0, keepdims=True)
        column = jnp.broadcast_to(weight, (n, n)).T
        for c in range(0, ref.shape[1], n):
            ref[:, c : c + n] = (total[i * n : (i + 1) * n, c : c + n] * column).astype(ref.dtype)
    for ref in kept:
        ref[...] = down_b[...]


def expert(blocks, kinds, choice, weights, n, keep=False):
    width = blocks[0].shape[1]
    out = [jax.ShapeDtypeStruct((n, width), kind) for kind in kinds]
    out += [jax.ShapeDtypeStruct(weights[3].shape, jnp.bfloat16)] * keep
    return pl.pallas_call(
        functools.partial(expert_kernel, len(blocks)),
        out_shape=out,
        in_specs=[pl.BlockSpec(memory_space=pltpu.VMEM)] * (len(blocks) + 5),
        out_specs=[pl.BlockSpec(memory_space=pltpu.VMEM)] * len(out),
        compiler_params=pltpu.CompilerParams(vmem_limit_bytes=24 << 20),
        cost_estimate=pl.CostEstimate(flops=n * width, bytes_accessed=n * width, transcendentals=0),
    )(*blocks, choice, *weights)


def gather_body(latent_rows, expert_ids, route_weights, up_weight, down_weight):
    groups = lax.axis_size("expert")
    n, width = latent_rows.shape
    me = lax.axis_index("expert")
    f32 = jnp.float32
    choice = jnp.broadcast_to((jnp.arange(groups) == me).astype(f32)[:, None], (groups, n))
    whole = pl.pallas_call(
        pack_kernel,
        out_shape=jax.ShapeDtypeStruct((n + groups, width), jnp.bfloat16),
        in_specs=[pl.BlockSpec(memory_space=pltpu.VMEM)] * 3,
        out_specs=pl.BlockSpec(memory_space=pltpu.VMEM),
    )(latent_rows, expert_ids.T, route_weights.T)
    near2 = across(whole, 4)
    far0 = across(whole, 1)
    near1 = across(whole, 2)
    weights = (up_weight[0], down_weight[0], other_core(up_weight[0]), other_core(down_weight[0]))
    far3 = across(near2, 3)
    near3 = across(near2, 2)
    far2 = across(near2, 1)
    far0 = after(far0, near2)
    bf16 = jnp.bfloat16
    own0, away0, kept = expert([whole, far0], [f32, bf16], choice, weights, n, keep=True)
    weights = weights[:3] + (kept,)
    far1 = across(after(far0, near2, away0), 2)
    near3, far2, far3 = lax.optimization_barrier((near3, far2, far3, away0, near1))[:3]
    away3, away2 = expert([far3, far2], [bf16, bf16], choice, weights, n)
    near3 = after(near3, away3)
    own3, own2 = expert([near3, near2], [f32, f32], choice, weights, n)
    near1 = after(near1, own3)
    own1, away1 = expert([near1, far1], [f32, bf16], choice, weights, n)

    def add(*terms):
        return functools.reduce(lambda a, b: a + b.astype(f32), terms).astype(jnp.bfloat16)

    over3 = across(away3, 1)
    over2 = across(away2, 1)
    over1 = across(away1, 1)
    over0 = across(after(away0, over2), 1)
    low3 = across(add(own3, over3), 2)
    sum2 = add(own2, over2, low3)
    high = across(sum2, 4)
    low1 = across(add(own1, after(over1, sum2)), 2)
    return add(own0, over0, low1, high)


def body(latent_rows, expert_ids, route_weights, up_weight, down_weight):
    groups = lax.axis_size("expert")
    rows_dev, choose = expert_ids.shape
    capacity = 3 * choose * rows_dev // (2 * groups)
    dense = groups == 8 and rows_dev <= 2 * capacity
    form = gather_body if dense else exchange_body
    return form(latent_rows, expert_ids, route_weights, up_weight, down_weight)


def solution(mesh):
    return jax.shard_map(
        body,
        mesh=mesh,
        in_specs=(
            P(("parts", "expert", "tensor"), None),
            P(("parts", "expert", "tensor"), None),
            P(("parts", "expert", "tensor"), None),
            P("expert", None, "tensor"),
            P("expert", "tensor", None),
        ),
        out_specs=P(("parts", "expert", "tensor"), None),
        check_vma=False,
    )
```

```python
import functools

import jax
import jax.numpy as jnp
from jax import lax
from jax.experimental import pallas as pl
from jax.experimental.pallas import tpu as pltpu
from jax.sharding import PartitionSpec as P


def exchange_body(latent_rows, expert_ids, route_weights, up_weight, down_weight):
    rows_dev = latent_rows.shape[0]
    width = latent_rows.shape[1]
    choose = expert_ids.shape[1]
    groups = lax.axis_size("expert")
    capacity = 3 * choose * rows_dev // (2 * groups)
    flat_ids = expert_ids.reshape(-1)
    onehot = (flat_ids[:, None] == jnp.arange(groups, dtype=jnp.int32)[None, :]).astype(jnp.int32)
    ranks = jnp.cumsum(onehot, axis=0) - onehot
    slots = jnp.sum(ranks * onehot, axis=1)
    target = flat_ids * capacity + slots
    repeated = jnp.repeat(latent_rows, choose, axis=0)
    outgoing = jnp.zeros((groups * capacity, width), jnp.bfloat16).at[target].set(repeated)
    outgoing = outgoing.reshape(groups, capacity, width)
    arrived = lax.all_to_all(outgoing, "expert", split_axis=0, concat_axis=0, tiled=True)
    arrived_rows = arrived.reshape(-1, width)
    both_rows = lax.all_gather(arrived_rows, "tensor", axis=0, tiled=True)
    pre = jnp.dot(both_rows, up_weight[0], preferred_element_type=jnp.float32)
    hidden = (jnp.maximum(pre, 0.0) ** 2).astype(jnp.bfloat16)
    partial_out = jnp.dot(hidden, down_weight[0], preferred_element_type=jnp.float32)
    summed = lax.psum_scatter(
        partial_out.astype(jnp.bfloat16), "tensor", scatter_dimension=0, tiled=True
    )
    returned = lax.all_to_all(
        summed.reshape(groups, capacity, width), "expert", split_axis=0, concat_axis=0, tiled=True
    )
    returned_rows = returned.reshape(-1, width)
    picked = returned_rows[target].astype(jnp.float32)
    weighted = picked * route_weights.reshape(-1)[:, None]
    combined = jnp.sum(weighted.reshape(rows_dev, choose, width), axis=1)
    return combined.astype(jnp.bfloat16)


def across(value, step):
    size = lax.axis_size("expert")
    return lax.ppermute(value, "expert", [(i, i ^ step) for i in range(size)])


def other_core(value):
    return lax.ppermute(value, "tensor", [(0, 1), (1, 0)])


def after(value, *others):
    return lax.optimization_barrier((value, *others))[0]


def pack_kernel(rows, ids, weights, out, strip):
    n, width = rows.shape
    lines = []
    for e in range(out.shape[0] - n):
        lines.append(jnp.sum(jnp.where(ids[...] == e, weights[...], 0.0), axis=0, keepdims=True))
    table = jnp.concatenate(lines, axis=0)
    high = table.astype(jnp.bfloat16)
    low = (table - high.astype(jnp.float32)).astype(jnp.bfloat16)
    rest = jnp.zeros((len(lines), width - 2 * n), jnp.bfloat16)
    strip[...] = jnp.concatenate([high, low], axis=1)
    out[...] = jnp.concatenate([rows[...], jnp.concatenate([high, low, rest], axis=1)], axis=0)


def expert_kernel(count, apart, *refs):
    f32 = jnp.float32
    blocks = [ref[...] for ref in refs[:count]]
    strips, refs = [ref[...] for ref in refs[count : count + apart]], refs[:count] + refs[count + apart :]
    choice, up_a, down_a, up_b, down_b = refs[count : count + 5]
    outs, kept = refs[count + 5 : 2 * count + 5], refs[2 * count + 5 :]
    n = outs[0].shape[0]
    rows = jnp.concatenate([b[:n] for b in blocks], axis=0)
    total = None
    for up, down in ((up_a, down_a), (up_b, down_b)):
        pre = jnp.dot(rows, up[...], preferred_element_type=f32)
        hidden = jnp.square(jnp.maximum(pre, 0.0)).astype(jnp.bfloat16)
        out = jnp.dot(hidden, down[...], preferred_element_type=f32)
        total = out if total is None else total + out
    for i, ref in enumerate(outs):
        pair = (strips[i] if strips else blocks[i][n:, : 2 * n]).astype(f32)
        weight = jnp.sum((pair[:, :n] + pair[:, n:]) * choice[...], axis=0, keepdims=True)
        column = jnp.broadcast_to(weight, (n, n)).T
        for c in range(0, ref.shape[1], n):
            ref[:, c : c + n] = (total[i * n : (i + 1) * n, c : c + n] * column).astype(ref.dtype)
    for ref in kept:
        ref[...] = down_b[...]


def expert(blocks, kinds, choice, weights, n, keep=False, strips=()):
    width = blocks[0].shape[1]
    out = [jax.ShapeDtypeStruct((n, width), kind) for kind in kinds]
    out += [jax.ShapeDtypeStruct(weights[3].shape, jnp.bfloat16)] * keep
    return pl.pallas_call(
        functools.partial(expert_kernel, len(blocks), len(strips)),
        out_shape=out,
        in_specs=[pl.BlockSpec(memory_space=pltpu.VMEM)] * (len(blocks) + len(strips) + 5),
        out_specs=[pl.BlockSpec(memory_space=pltpu.VMEM)] * len(out),
        compiler_params=pltpu.CompilerParams(vmem_limit_bytes=24 << 20),
        cost_estimate=pl.CostEstimate(flops=n * width, bytes_accessed=n * width, transcendentals=0),
    )(*blocks, *strips, choice, *weights)


def gather_body(latent_rows, expert_ids, route_weights, up_weight, down_weight):
    groups = lax.axis_size("expert")
    n, width = latent_rows.shape
    me = lax.axis_index("expert")
    f32 = jnp.float32
    choice = jnp.broadcast_to((jnp.arange(groups) == me).astype(f32)[:, None], (groups, n))
    whole, strip = pl.pallas_call(
        pack_kernel,
        out_shape=[
            jax.ShapeDtypeStruct((n + groups, width), jnp.bfloat16),
            jax.ShapeDtypeStruct((groups, 2 * n), jnp.bfloat16),
        ],
        in_specs=[pl.BlockSpec(memory_space=pltpu.VMEM)] * 3,
        out_specs=[pl.BlockSpec(memory_space=pltpu.VMEM)] * 2,
    )(latent_rows, expert_ids.T, route_weights.T)
    near2 = across(latent_rows, 4)
    strip2 = across(strip, 4)
    far0 = across(whole, 1)
    near1 = across(whole, 2)
    weights = (up_weight[0], down_weight[0], other_core(up_weight[0]), other_core(down_weight[0]))
    bf16 = jnp.bfloat16
    own0, kept = expert([whole], [f32], choice, weights, n, keep=True)
    near2 = after(near2, own0)
    far3 = across(near2, 3)
    near3 = across(near2, 2)
    far2 = across(near2, 1)
    line = after(strip2, near2)
    line3far, line3, line2far = [across(line, step) for step in (3, 2, 1)]
    weights = weights[:3] + (kept,)
    far0 = after(far0, near2)
    (away0,) = expert([far0], [bf16], choice, weights, n)
    far1 = across(after(far0, near2, away0), 2)
    near3, far2, far3 = lax.optimization_barrier((near3, far2, far3, away0, near1))[:3]
    away3, away2 = expert([far3, far2], [bf16, bf16], choice, weights, n, strips=[line3far, line2far])
    near3 = after(near3, away3)
    own3, own2 = expert([near3, near2], [f32, f32], choice, weights, n, strips=[line3, strip2])
    near1 = after(near1, own3)
    own1, away1 = expert([near1, far1], [f32, bf16], choice, weights, n)

    def add(*terms):
        return functools.reduce(lambda a, b: a + b.astype(f32), terms).astype(jnp.bfloat16)

    over3 = across(away3, 1)
    over2 = across(away2, 1)
    over1 = across(away1, 1)
    over0 = across(after(away0, over2), 1)
    low3 = across(add(own3, over3), 2)
    sum2 = add(own2, over2, low3)
    high = across(sum2, 4)
    low1 = across(add(own1, after(over1, sum2)), 2)
    return add(own0, over0, low1, high)


def body(latent_rows, expert_ids, route_weights, up_weight, down_weight):
    groups = lax.axis_size("expert")
    rows_dev, choose = expert_ids.shape
    capacity = 3 * choose * rows_dev // (2 * groups)
    dense = groups == 8 and rows_dev <= 2 * capacity
    form = gather_body if dense else exchange_body
    return form(latent_rows, expert_ids, route_weights, up_weight, down_weight)


def solution(mesh):
    return jax.shard_map(
        body,
        mesh=mesh,
        in_specs=(
            P(("parts", "expert", "tensor"), None),
            P(("parts", "expert", "tensor"), None),
            P(("parts", "expert", "tensor"), None),
            P("expert", None, "tensor"),
            P("expert", "tensor", None),
        ),
        out_specs=P(("parts", "expert", "tensor"), None),
        check_vma=False,
    )
```

```python
import functools

import jax
import jax.numpy as jnp
from jax import lax
from jax.experimental import pallas as pl
from jax.experimental.pallas import tpu as pltpu
from jax.sharding import PartitionSpec as P


def exchange_body(latent_rows, expert_ids, route_weights, up_weight, down_weight):
    rows_dev = latent_rows.shape[0]
    width = latent_rows.shape[1]
    choose = expert_ids.shape[1]
    groups = lax.axis_size("expert")
    capacity = 3 * choose * rows_dev // (2 * groups)
    flat_ids = expert_ids.reshape(-1)
    onehot = (flat_ids[:, None] == jnp.arange(groups, dtype=jnp.int32)[None, :]).astype(jnp.int32)
    ranks = jnp.cumsum(onehot, axis=0) - onehot
    slots = jnp.sum(ranks * onehot, axis=1)
    target = flat_ids * capacity + slots
    repeated = jnp.repeat(latent_rows, choose, axis=0)
    outgoing = jnp.zeros((groups * capacity, width), jnp.bfloat16).at[target].set(repeated)
    outgoing = outgoing.reshape(groups, capacity, width)
    arrived = lax.all_to_all(outgoing, "expert", split_axis=0, concat_axis=0, tiled=True)
    arrived_rows = arrived.reshape(-1, width)
    both_rows = lax.all_gather(arrived_rows, "tensor", axis=0, tiled=True)
    pre = jnp.dot(both_rows, up_weight[0], preferred_element_type=jnp.float32)
    hidden = (jnp.maximum(pre, 0.0) ** 2).astype(jnp.bfloat16)
    partial_out = jnp.dot(hidden, down_weight[0], preferred_element_type=jnp.float32)
    summed = lax.psum_scatter(
        partial_out.astype(jnp.bfloat16), "tensor", scatter_dimension=0, tiled=True
    )
    returned = lax.all_to_all(
        summed.reshape(groups, capacity, width), "expert", split_axis=0, concat_axis=0, tiled=True
    )
    returned_rows = returned.reshape(-1, width)
    picked = returned_rows[target].astype(jnp.float32)
    weighted = picked * route_weights.reshape(-1)[:, None]
    combined = jnp.sum(weighted.reshape(rows_dev, choose, width), axis=1)
    return combined.astype(jnp.bfloat16)


def across(value, step):
    size = lax.axis_size("expert")
    return lax.ppermute(value, "expert", [(i, i ^ step) for i in range(size)])


def other_core(value):
    return lax.ppermute(value, "tensor", [(0, 1), (1, 0)])


def after(value, *others):
    return lax.optimization_barrier((value, *others))[0]


def pack_kernel(rows, ids, weights, out, strip):
    n, width = rows.shape
    lines = []
    for e in range(out.shape[0] - n):
        lines.append(jnp.sum(jnp.where(ids[...] == e, weights[...], 0.0), axis=0, keepdims=True))
    table = jnp.concatenate(lines, axis=0)
    high = table.astype(jnp.bfloat16)
    low = (table - high.astype(jnp.float32)).astype(jnp.bfloat16)
    rest = jnp.zeros((len(lines), width - 2 * n), jnp.bfloat16)
    strip[...] = jnp.concatenate([high, low], axis=1)
    out[...] = jnp.concatenate([rows[...], jnp.concatenate([high, low, rest], axis=1)], axis=0)


def expert_kernel(count, apart, *refs):
    f32 = jnp.float32
    blocks = [ref[...] for ref in refs[:count]]
    strips, refs = [ref[...] for ref in refs[count : count + apart]], refs[:count] + refs[count + apart :]
    choice, up_a, down_a, up_b, down_b = refs[count : count + 5]
    outs, kept = refs[count + 5 : 2 * count + 5], refs[2 * count + 5 :]
    n = outs[0].shape[0]
    rows = jnp.concatenate([b[:n] for b in blocks], axis=0)
    total = None
    for up, down in ((up_a, down_a), (up_b, down_b)):
        pre = jnp.dot(rows, up[...], preferred_element_type=f32)
        hidden = jnp.square(jnp.maximum(pre, 0.0)).astype(jnp.bfloat16)
        out = jnp.dot(hidden, down[...], preferred_element_type=f32)
        total = out if total is None else total + out
    for i, ref in enumerate(outs):
        pair = (strips[i] if strips else blocks[i][n:, : 2 * n]).astype(f32)
        weight = jnp.sum((pair[:, :n] + pair[:, n:]) * choice[...], axis=0, keepdims=True)
        column = jnp.broadcast_to(weight, (n, n)).T
        for c in range(0, ref.shape[1], n):
            ref[:, c : c + n] = (total[i * n : (i + 1) * n, c : c + n] * column).astype(ref.dtype)
    for ref in kept:
        ref[...] = down_b[...]


def expert(blocks, kinds, choice, weights, n, keep=False, strips=()):
    width = blocks[0].shape[1]
    out = [jax.ShapeDtypeStruct((n, width), kind) for kind in kinds]
    out += [jax.ShapeDtypeStruct(weights[3].shape, jnp.bfloat16)] * keep
    return pl.pallas_call(
        functools.partial(expert_kernel, len(blocks), len(strips)),
        out_shape=out,
        in_specs=[pl.BlockSpec(memory_space=pltpu.VMEM)] * (len(blocks) + len(strips) + 5),
        out_specs=[pl.BlockSpec(memory_space=pltpu.VMEM)] * len(out),
        compiler_params=pltpu.CompilerParams(vmem_limit_bytes=24 << 20),
        cost_estimate=pl.CostEstimate(flops=n * width, bytes_accessed=n * width, transcendentals=0),
    )(*blocks, *strips, choice, *weights)


def gather_body(latent_rows, expert_ids, route_weights, up_weight, down_weight):
    groups = lax.axis_size("expert")
    n, width = latent_rows.shape
    me = lax.axis_index("expert")
    f32 = jnp.float32
    choice = jnp.broadcast_to((jnp.arange(groups) == me).astype(f32)[:, None], (groups, n))
    whole, strip = pl.pallas_call(
        pack_kernel,
        out_shape=[
            jax.ShapeDtypeStruct((n + groups, width), jnp.bfloat16),
            jax.ShapeDtypeStruct((groups, 2 * n), jnp.bfloat16),
        ],
        in_specs=[pl.BlockSpec(memory_space=pltpu.VMEM)] * 3,
        out_specs=[pl.BlockSpec(memory_space=pltpu.VMEM)] * 2,
    )(latent_rows, expert_ids.T, route_weights.T)
    near2 = across(latent_rows, 4)
    strip2 = across(strip, 4)
    far0 = across(whole, 1)
    near1 = across(whole, 2)
    weights = (up_weight[0], down_weight[0], other_core(up_weight[0]), other_core(down_weight[0]))
    bf16 = jnp.bfloat16
    own0, kept = expert([whole], [f32], choice, weights, n, keep=True)
    near2 = after(near2, own0)
    far3 = across(near2, 3)
    near3 = across(near2, 2)
    far2 = across(near2, 1)
    line = after(strip2, near2)
    line3far, line3, line2far = [across(line, step) for step in (3, 2, 1)]
    weights = weights[:3] + (kept,)
    far0 = after(far0, near2)
    (away0,) = expert([far0], [bf16], choice, weights, n)
    far1 = across(after(far0, near2, away0), 2)
    near3, far2, far3 = lax.optimization_barrier((near3, far2, far3, away0, near1))[:3]
    far3 = after(far3, line2far)
    (away3,) = expert([far3], [bf16], choice, weights, n, strips=[line3far])
    far2 = after(far2, away3)
    (away2,) = expert([far2], [bf16], choice, weights, n, strips=[line2far])
    near3 = after(near3, away2)
    own3, own2 = expert([near3, near2], [f32, f32], choice, weights, n, strips=[line3, strip2])
    near1 = after(near1, own3)
    own1, away1 = expert([near1, far1], [f32, bf16], choice, weights, n)

    def add(*terms):
        return functools.reduce(lambda a, b: a + b.astype(f32), terms).astype(jnp.bfloat16)

    over3 = across(away3, 1)
    over2 = across(away2, 1)
    over1 = across(away1, 1)
    over0 = across(after(away0, over2), 1)
    low3 = across(add(own3, over3), 2)
    sum2 = add(own2, over2, low3)
    high = across(sum2, 4)
    low1 = across(add(own1, after(over1, sum2)), 2)
    return add(own0, over0, low1, high)


def body(latent_rows, expert_ids, route_weights, up_weight, down_weight):
    groups = lax.axis_size("expert")
    rows_dev, choose = expert_ids.shape
    capacity = 3 * choose * rows_dev // (2 * groups)
    dense = groups == 8 and rows_dev <= 2 * capacity
    form = gather_body if dense else exchange_body
    return form(latent_rows, expert_ids, route_weights, up_weight, down_weight)


def solution(mesh):
    return jax.shard_map(
        body,
        mesh=mesh,
        in_specs=(
            P(("parts", "expert", "tensor"), None),
            P(("parts", "expert", "tensor"), None),
            P(("parts", "expert", "tensor"), None),
            P("expert", None, "tensor"),
            P("expert", "tensor", None),
        ),
        out_specs=P(("parts", "expert", "tensor"), None),
        check_vma=False,
    )
```
